256 devices in a mesh: silo: 16 (over y, x), feat: 16 (over z, core).
Axes of the slice: x: 4, y: 4, z: 8, core: 2. Of those that a mesh axis runs over, the one named last changes fastest.
Arguments:
- samples: bfloat16 [8192, 131072], P('silo', 'feat'), may hold values from -6 to 6
- components: bfloat16 [64, 131072], P(None, 'feat'), may hold values from -0.015625 to 0.015625
- row_counts: int32 [16], P('silo'), may hold values from 128 to 512, as said below
- observed: int32 [16, 256], P('silo', 'feat'), may hold values from 0 to 1, as said below
- block_owner: int32 [256], P('feat'), may hold values from 0 to 15, as said below
Outputs:
- grad_owned: float32 [64, 131072], P(None, ('silo', 'feat'))
The draws below stay inside these ranges and needn't reach their ends.
Inputs may be any that keep to these rules, and one draw needn't show every extreme that they name: `row_counts`: one silo has all 512 row slots used in every draw. `observed`: every entry is 0 or 1, and at least one entry is 1 (some silo observes some block). `block_owner`: each silo owns exactly 1 block of every slice of 16 blocks.
All inputs are finite; a program needn't handle non-finite values.
Results may differ from the reference program's by a relative error of at most 0.0029.
Values sent between devices are 32-bit elements; how exact they have to be, the bound alone decides.
A program may use at most 64 MiB of HBM per device.

```python
import jax
import jax.numpy as jnp
from jax import lax

K = 64
BLOCK = 512
ROWS_DEV = 512
F = 131072
ROWS = 8192
BLOCKS_DEV = 16
OWN = 1
N_SILO = 16
N_FEAT = 16


def owner_layout(key):
    base_list = jnp.repeat(jnp.arange(N_SILO, dtype=jnp.int32), OWN)
    slice_keys = jax.random.split(jax.random.fold_in(key, 11), N_FEAT)
    return jax.vmap(lambda one_key: jax.random.permutation(one_key, base_list))(slice_keys)


def draw_block_owner(key, part):
    return owner_layout(key).reshape(N_FEAT * BLOCKS_DEV).astype(jnp.int32)


def draw_observed(key, part):
    layout = owner_layout(key)
    key = jax.random.fold_in(key, 5)
    key_flag, key_pick = jax.random.split(key)
    flags = jax.random.randint(key_flag, (N_SILO, N_FEAT, N_SILO), 0, 2)
    flags = flags.at[0, 0, 0].set(1)
    picks = jax.random.randint(key_pick, (N_SILO, N_FEAT, N_SILO), 0, OWN)
    block_idx = jnp.arange(BLOCKS_DEV, dtype=jnp.int32)
    same_owner = layout[:, :, None] == layout[:, None, :]
    earlier = block_idx[None, :] < block_idx[:, None]
    position = jnp.sum(same_owner & earlier[None, :, :], axis=2).astype(jnp.int32)
    feat_idx = jnp.arange(N_FEAT, dtype=jnp.int32)[:, None]
    flag_block = flags[:, feat_idx, layout]
    pick_block = picks[:, feat_idx, layout]
    seen = (flag_block == 1) & (pick_block == position[None, :, :])
    return seen.astype(jnp.int32).reshape(N_SILO, N_FEAT * BLOCKS_DEV)


def draw_row_counts(key, part):
    key = jax.random.fold_in(key, 7)
    key_count, key_busy = jax.random.split(key)
    counts = jax.random.randint(key_count, (N_SILO,), ROWS_DEV // 4, ROWS_DEV // 2 + 1)
    busiest = jax.random.randint(key_busy, (), 0, N_SILO)
    return jnp.where(jnp.arange(N_SILO, dtype=jnp.int32) == busiest, ROWS_DEV, counts).astype(jnp.int32)


def block_scale(stream_key, dims, pieces, least, top_value):
    gain, own = 1.0, jax.random.fold_in(stream_key, 6)
    for dim, blocks in pieces:
        heights = jnp.exp(jax.random.uniform(jax.random.fold_in(own, dim), (blocks,), jnp.float32, least / len(pieces), top_value / len(pieces)))
        gain = gain * jnp.repeat(heights, dims[dim] // blocks).reshape([-1 if axis == dim else 1 for axis in range(len(dims))])
    return gain


def scatter_about(stream_key, dims, scale, bound, cuts=(), held_as=jnp.bfloat16):
    array = jax.random.normal(stream_key, dims, jnp.float32) * scale
    if len(cuts) > 0:
        array = block_scale(stream_key, dims, cuts, -0.22, 0.18) * array
    return jnp.clip(array, min=-bound, max=bound).astype(held_as)


def setup_inputs(seed: int = 0) -> dict:
    splits = jax.random.split(jax.random.key(seed), 6)
    return {
        "samples": scatter_about(splits[0], (ROWS, F), 1.0, 6.0, ((0, 16), (1, 16))),
        "components": scatter_about(splits[1], (K, F), F ** -0.5, 0.015625, ((1, 16),)),
        "row_counts": draw_row_counts(jax.random.fold_in(splits[5], 71), 0),
        "observed": draw_observed(jax.random.fold_in(splits[5], 71), 0),
        "block_owner": draw_block_owner(jax.random.fold_in(splits[5], 71), 0),
    }


def reference(samples, components, row_counts, observed, block_owner):
    gram_matrix = jnp.dot(components, components.T, preferred_element_type=jnp.float32)
    comp_wide = components.astype(jnp.float32)
    slot_index = jnp.arange(ROWS_DEV, dtype=jnp.int32)

    def per_silo(carry, silo_idx):
        accum, cross_sum = carry
        sample_block = lax.dynamic_slice_in_dim(samples, silo_idx * ROWS_DEV, ROWS_DEV, 0)
        seen_row = lax.dynamic_index_in_dim(observed, silo_idx, 0, keepdims=False)
        col_mask = jnp.repeat(seen_row, BLOCK).astype(jnp.bfloat16)
        count_here = lax.dynamic_index_in_dim(row_counts, silo_idx, 0, keepdims=False)
        row_mask = (slot_index < count_here).astype(jnp.bfloat16)
        masked = sample_block * row_mask[:, None] * col_mask[None, :]
        projected = jnp.dot(masked, components.T, preferred_element_type=jnp.float32)
        proj_bf = projected.astype(jnp.bfloat16)
        partial_value = jnp.dot(proj_bf.T, masked, preferred_element_type=jnp.float32)
        accum = accum + partial_value
        cross_sum = cross_sum + jnp.dot(projected.T, projected, precision=lax.Precision.HIGHEST)
        return (accum, cross_sum), None

    start = (jnp.zeros((K, F), jnp.float32), jnp.zeros((K, K), jnp.float32))
    (accum, cross_sum), _ = lax.scan(per_silo, start, jnp.arange(N_SILO, dtype=jnp.int32))
    row_total = jnp.sum(row_counts).astype(jnp.float32)
    factor = 2.0 * jnp.eye(K, dtype=jnp.float32) - gram_matrix
    full_grad = jnp.dot(factor, accum, precision=lax.Precision.HIGHEST) - jnp.dot(cross_sum, comp_wide, precision=lax.Precision.HIGHEST)
    full_grad = (-2.0 / row_total) * full_grad
    owners = block_owner.reshape(N_FEAT, BLOCKS_DEV)
    sort_keys = owners * BLOCKS_DEV + jnp.arange(BLOCKS_DEV, dtype=jnp.int32)[None, :]
    block_order = jnp.argsort(sort_keys, axis=1).astype(jnp.int32)
    blocked = full_grad.reshape(K, N_FEAT, BLOCKS_DEV, BLOCK)
    arranged = jnp.take_along_axis(blocked, block_order[None, :, :, None], axis=2)
    arranged = arranged.reshape(K, N_FEAT, N_SILO, OWN, BLOCK).transpose(0, 2, 1, 3, 4)
    return arranged.reshape(K, F)
```

```python
import jax
import jax.numpy as jnp
from jax import lax
from jax.experimental import pallas as pl
from jax.experimental.pallas import tpu as pltpu
from jax.sharding import PartitionSpec as P

MESH = pl.DeviceIdType.MESH
F32 = jnp.float32
BF16 = jnp.bfloat16
HIGHEST = lax.Precision.HIGHEST
SIDE = 4
NF = 16
NB = 16
W = 512
HALF = 256
ROWS = 512
K = 64
CH = 18


def dot_nt(a, b, precision=None):
    return lax.dot_general(
        a, b, (((1,), (1,)), ((), ())), precision=precision, preferred_element_type=F32
    )


def dot_nn(a, b):
    return jnp.dot(a, b, preferred_element_type=F32)


def dot_tn(a, b, precision=None):
    return lax.dot_general(
        a, b, (((0,), (0,)), ((), ())), precision=precision, preferred_element_type=F32
    )


def kernel(
    samples, components, counts, observed, owner, out,
    xv, acc, sbuf, r1, g2, gp, inv, lhs, lhs_c, cnt, cnt_r,
    ta, tb, ra, rb, sa, sb, r2a, r2b,
    ld_sem, s1_s, s1_r, s2_s, s2_r, c_s, c_r,
    a1_s, a1_r, b1_s, b1_r, a2_s, a2_r, b2_s, b2_r,
):
    silo = lax.axis_index("silo")
    f = lax.axis_index("feat")
    y, x = silo // SIDE, silo % SIDE

    def feat_dev(off):
        return (silo, lax.rem(f + off, NF))

    def silo_dev(dy, dx):
        return (lax.rem(y + dy, SIDE) * SIDE + lax.rem(x + dx, SIDE), f)

    def loads(b):
        cols = pl.ds(pl.multiple_of(b * W, W), W)
        return (
            pltpu.make_async_copy(samples.at[:, cols], xv.at[b, pl.ds(0, ROWS)], ld_sem.at[b, 0]),
            pltpu.make_async_copy(components.at[:, cols], xv.at[b, pl.ds(ROWS, K)], ld_sem.at[b, 1]),
            pltpu.make_async_copy(components.at[:, cols], xv.at[b, pl.ds(ROWS + K, K)], ld_sem.at[b, 2]),
        )

    barrier = pltpu.get_barrier_semaphore()
    for off in range(1, NF):
        pl.semaphore_signal(barrier, inc=1, device_id=feat_dev(off), device_id_type=MESH)
    for k in range(1, SIDE):
        pl.semaphore_signal(barrier, inc=1, device_id=silo_dev(0, k), device_id_type=MESH)
        pl.semaphore_signal(barrier, inc=1, device_id=silo_dev(k, 0), device_id_type=MESH)

    def start_load(b, c):
        for cp in loads(b):
            cp.start()
        return c

    lax.fori_loop(0, NB, start_load, 0)

    def invert(d, c):
        total = jnp.int32(0)
        for b in range(NB):
            total = jnp.where(owner[b] == d, jnp.int32(b), total)
        inv[d] = total
        return c

    lax.fori_loop(0, NB, invert, 0)
    cnt[0] = jnp.full((8, 128), counts[0].astype(F32), F32)

    acc[...] = jnp.zeros_like(acc)
    left = lax.broadcasted_iota(jnp.int32, (HALF, 128), 1) < K
    left_g = lax.broadcasted_iota(jnp.int32, (32, 128), 1) < K

    def project(b, c):
        for cp in loads(b):
            cp.wait()
        seen = observed[0, b].astype(F32)
        r = dot_nt(xv[b, 0 : ROWS + K, :], xv[b, ROWS : ROWS + 2 * K, :])
        acc[0:HALF, :] += seen * jnp.where(left, r[0:HALF], r[HALF:ROWS])
        acc[HALF : HALF + 32, :] += jnp.where(
            left_g, r[ROWS : ROWS + 32], r[ROWS + 32 : ROWS + 64]
        )
        return c

    lax.fori_loop(0, NB, project, 0)

    for j in range(NF):
        sbuf[j, 0:16, :] = acc[16 * j : 16 * j + 16, :]
        sbuf[j, 16:18, :] = acc[HALF + 2 * j : HALF + 2 * j + 2, :]

    pl.semaphore_wait(barrier, NF - 1 + 2 * (SIDE - 1))

    def rs_copy(off):
        peer = lax.rem(f + off, NF)
        return pltpu.make_async_remote_copy(
            src_ref=sbuf.at[peer], dst_ref=r1.at[off], send_sem=s1_s.at[off],
            recv_sem=s1_r.at[off], device_id=(silo, peer), device_id_type=MESH,
        )

    order = [8, 9, 7, 6, 10, 11, 5, 4, 12, 13, 3, 2, 14, 15, 1]
    for off in order:
        rs_copy(off).start()

    def cnt_copy(k, stage):
        dev = silo_dev(0, k) if stage == 0 else silo_dev(k, 0)
        return pltpu.make_async_remote_copy(
            src_ref=cnt.at[stage], dst_ref=cnt_r.at[stage, k], send_sem=c_s.at[stage, k],
            recv_sem=c_r.at[stage, k], device_id=dev, device_id_type=MESH,
        )

    for k in range(1, SIDE):
        cnt_copy(k, 0).start()

    total = sbuf[f]
    for off in range(1, NF):
        rs_copy(off).wait_recv()
        total = total + r1[off]
    g2[f] = total

    def ag_copy(off):
        return pltpu.make_async_remote_copy(
            src_ref=g2.at[f], dst_ref=g2.at[f], send_sem=s2_s.at[off],
            recv_sem=s2_r.at[off], device_id=feat_dev(off), device_id_type=MESH,
        )

    for off in order:
        ag_copy(off).start()

    for k in range(1, SIDE):
        cnt_copy(k, 0).wait_recv()
    cnt[1] = cnt[0] + cnt_r[0, 1] + cnt_r[0, 2] + cnt_r[0, 3]
    for k in range(1, SIDE):
        cnt_copy(k, 1).start()

    for off in range(1, NF):
        ag_copy(off).wait_recv()

    used = counts[0]
    lane = lax.broadcasted_iota(jnp.int32, (HALF, 128), 1)
    row = lax.broadcasted_iota(jnp.int32, (HALF, 128), 0)
    row = row + jnp.where(lane >= K, HALF, 0)
    proj = g2[:, 0:16, :].reshape(HALF, 128)
    proj = jnp.where(row < used, proj, 0.0)
    for j in range(NF):
        gp[2 * j : 2 * j + 2, :] = g2[j, 16:18, :]
    gram = gp[...]
    gram_r = pltpu.roll(gram, K, 1)
    zero = jnp.zeros_like(gram)
    factor = jnp.concatenate(
        [
            jnp.where(left_g, gram, zero), jnp.where(left_g, gram_r, zero),
            jnp.where(left_g, zero, gram_r), jnp.where(left_g, zero, gram),
        ],
        axis=0,
    )
    r_i = lax.broadcasted_iota(jnp.int32, (128, 128), 0)
    c_i = lax.broadcasted_iota(jnp.int32, (128, 128), 1)
    factor = jnp.where(r_i == c_i, 2.0, 0.0) - factor
    q = dot_nt(factor, proj.astype(BF16).astype(F32), HIGHEST)
    q_hi = q.astype(BF16)
    q_lo = (q - q_hi.astype(F32)).astype(BF16)
    lhs[0:K, 0:HALF] = q_hi[0:K]
    lhs[K : 2 * K, 0:HALF] = q_lo[0:K]
    lhs[0:K, HALF:ROWS] = q_hi[K : 2 * K]
    lhs[K : 2 * K, HALF:ROWS] = q_lo[K : 2 * K]
    cross = dot_tn(proj, proj, HIGHEST)
    left_k = lax.broadcasted_iota(jnp.int32, (K, 128), 1) < K
    top, bottom = cross[0:K], cross[K : 2 * K]
    cross = jnp.where(left_k, top, bottom) + jnp.where(
        left_k, pltpu.roll(bottom, K, 1), pltpu.roll(top, K, 1)
    )
    c_hi = cross.astype(BF16).astype(F32)
    c_lo = cross - c_hi
    lhs_c[...] = jnp.where(left_k, -c_hi, -c_lo).astype(BF16)

    def half_block(dy, dx, cols):
        d = lax.rem(y + dy, SIDE) * SIDE + lax.rem(x + dx, SIDE)
        b = inv[d]
        seen = observed[0, b].astype(F32)
        p = dot_nn(lhs[...], xv[b, 0:ROWS, cols])
        return seen * (p[0:K] + p[K : 2 * K]) + dot_nn(
            lhs_c[...], xv[b, ROWS : ROWS + 2 * K, cols]
        )

    ca, cb = slice(0, HALF), slice(HALF, W)

    def a1_copy(k, i):
        return pltpu.make_async_remote_copy(
            src_ref=ta.at[k, i], dst_ref=ra.at[k, i], send_sem=a1_s.at[k, i],
            recv_sem=a1_r.at[k, i], device_id=silo_dev(0, k), device_id_type=MESH,
        )

    def b1_copy(k, i):
        return pltpu.make_async_remote_copy(
            src_ref=tb.at[k, i], dst_ref=rb.at[k, i], send_sem=b1_s.at[k, i],
            recv_sem=b1_r.at[k, i], device_id=silo_dev(k, 0), device_id_type=MESH,
        )

    def first(n, c):
        k = lax.rem(n // SIDE + 1, SIDE - 1) + 1
        i = lax.rem(n, SIDE)
        ta[k, i] = half_block(i, k, ca)
        a1_copy(k, i).start()
        tb[k, i] = half_block(k, i, cb)
        b1_copy(k, i).start()
        return c

    lax.fori_loop(0, SIDE * (SIDE - 1), first, 0)

    def own(i, c):
        ta[0, i] = half_block(i, 0, ca)
        tb[0, i] = half_block(0, i, cb)
        return c

    lax.fori_loop(0, SIDE, own, 0)

    def a2_copy(k):
        return pltpu.make_async_remote_copy(
            src_ref=sa.at[k], dst_ref=r2a.at[k], send_sem=a2_s.at[k],
            recv_sem=a2_r.at[k], device_id=silo_dev(k, 0), device_id_type=MESH,
        )

    def b2_copy(k):
        return pltpu.make_async_remote_copy(
            src_ref=sb.at[k], dst_ref=r2b.at[k], send_sem=b2_s.at[k],
            recv_sem=b2_r.at[k], device_id=silo_dev(0, k), device_id_type=MESH,
        )

    for i in (2, 3, 1, 0):
        for k in range(1, SIDE):
            a1_copy(k, i).wait_recv()
        sa[i] = ta[0, i] + ra[1, i] + ra[2, i] + ra[3, i]
        if i:
            a2_copy(i).start()
        for k in range(1, SIDE):
            b1_copy(k, i).wait_recv()
        sb[i] = tb[0, i] + rb[1, i] + rb[2, i] + rb[3, i]
        if i:
            b2_copy(i).start()

    for k in range(1, SIDE):
        cnt_copy(k, 1).wait_recv()
    rows = cnt[1] + cnt_r[1, 1] + cnt_r[1, 2] + cnt_r[1, 3]
    scale = -2.0 / rows[0:1, 0:1]
    for k in range(1, SIDE):
        a2_copy(k).wait_recv()
        b2_copy(k).wait_recv()
    out[:, 0:HALF] = scale * (sa[0] + r2a[1] + r2a[2] + r2a[3])
    out[:, HALF:W] = scale * (sb[0] + r2b[1] + r2b[2] + r2b[3])

    for off in range(1, NF):
        rs_copy(off).wait_send()
        ag_copy(off).wait_send()
    for k in range(1, SIDE):
        cnt_copy(k, 0).wait_send()
        cnt_copy(k, 1).wait_send()
        a2_copy(k).wait_send()
        b2_copy(k).wait_send()
        for i in range(SIDE):
            a1_copy(k, i).wait_send()
            b1_copy(k, i).wait_send()


def local(samples, components, row_counts, observed, block_owner):
    dma = pltpu.SemaphoreType.DMA
    return pl.pallas_call(
        kernel,
        name="pca_grad",
        out_shape=jax.ShapeDtypeStruct((K, W), F32),
        in_specs=[
            pl.BlockSpec(memory_space=pl.ANY),
            pl.BlockSpec(memory_space=pl.ANY),
            pl.BlockSpec(memory_space=pltpu.SMEM),
            pl.BlockSpec(memory_space=pltpu.SMEM),
            pl.BlockSpec(memory_space=pltpu.SMEM),
        ],
        out_specs=pl.BlockSpec(memory_space=pltpu.VMEM),
        scratch_shapes=[
            pltpu.VMEM((NB, ROWS + 2 * K, W), BF16),
            pltpu.VMEM((HALF + 32, 128), F32),
            pltpu.VMEM((NF, CH, 128), F32),
            pltpu.VMEM((NF, CH, 128), F32),
            pltpu.VMEM((NF, CH, 128), F32),
            pltpu.VMEM((32, 128), F32),
            pltpu.SMEM((NB,), jnp.int32),
            pltpu.VMEM((2 * K, ROWS), BF16),
            pltpu.VMEM((K, 128), BF16),
            pltpu.VMEM((2, 8, 128), F32),
            pltpu.VMEM((2, SIDE, 8, 128), F32),
            pltpu.VMEM((SIDE, SIDE, K, HALF), F32),
            pltpu.VMEM((SIDE, SIDE, K, HALF), F32),
            pltpu.VMEM((SIDE, SIDE, K, HALF), F32),
            pltpu.VMEM((SIDE, SIDE, K, HALF), F32),
            pltpu.VMEM((SIDE, K, HALF), F32),
            pltpu.VMEM((SIDE, K, HALF), F32),
            pltpu.VMEM((SIDE, K, HALF), F32),
            pltpu.VMEM((SIDE, K, HALF), F32),
            dma((NB, 3)),
            dma((NF,)), dma((NF,)), dma((NF,)), dma((NF,)),
            dma((2, SIDE)), dma((2, SIDE)),
            dma((SIDE, SIDE)), dma((SIDE, SIDE)),
            dma((SIDE, SIDE)), dma((SIDE, SIDE)),
            dma((SIDE,)), dma((SIDE,)), dma((SIDE,)), dma((SIDE,)),
        ],
        compiler_params=pltpu.CompilerParams(
            collective_id=0, has_side_effects=True, vmem_limit_bytes=40 * 2**20
        ),
        cost_estimate=pl.CostEstimate(
            flops=4 * ROWS * K * NB * W, bytes_accessed=10 * 2**20, transcendentals=0
        ),
    )(samples, components, row_counts, observed, block_owner)


def solution(mesh):
    in_specs = (P("silo", "feat"), P(None, "feat"), P("silo"), P("silo", "feat"), P("feat"))
    out_specs = P(None, ("silo", "feat"))
    return jax.shard_map(local, mesh=mesh, in_specs=in_specs, out_specs=out_specs, check_vma=False)
```

```python
import jax
import jax.numpy as jnp
from jax import lax
from jax.experimental import pallas as pl
from jax.experimental.pallas import tpu as pltpu
from jax.sharding import PartitionSpec as P

MESH = pl.DeviceIdType.MESH
F32 = jnp.float32
BF16 = jnp.bfloat16
SIDE = 4
NF = 16
NB = 16
W = 512
HALF = 256
ROWS = 512
K = 64
RK = ROWS + K
KC = K // NF
CW = 640
GROUP = 4

FAR_FIRST = [8, 9, 7, 6, 10, 11, 5, 4, 12, 13, 3, 2, 14, 15, 1]
BLOCKS = [
    (2, 2), (3, 2), (2, 3), (1, 2), (2, 1), (0, 2), (2, 0), (3, 1),
    (1, 3), (0, 1), (1, 0), (3, 3), (1, 1), (0, 3), (3, 0), (0, 0),
]
WAY = {2: 1, 1: 1, 3: SIDE - 1, 0: SIDE - 1}


def dot_nt(a, b):
    return lax.dot_general(a, b, (((1,), (1,)), ((), ())), preferred_element_type=F32)


def dot_nn(a, b):
    return jnp.dot(a, b, preferred_element_type=F32)


def split(v, terms):
    out = []
    for _ in range(terms):
        t = v.astype(BF16)
        out.append(t)
        v = v - t.astype(F32)
    return out


def kernel(
    samples, components, counts, observed_in, owner_in, out,
    observed, owner, xv, acc, sbuf, r1, g2, inv, lhs, cnt, cnt_r,
    ta, tb, ra, rb, sa, sb, r2a, r2b,
    in_sem, ld_sem, s1_s, s1_r, s2_s, s2_r, c_s, c_r,
    a_s, a_r, b_s, b_r, a2_s, a2_r, b2_s, b2_r,
):
    silo = lax.axis_index("silo")
    f = lax.axis_index("feat")
    y, x = silo // SIDE, silo % SIDE

    def feat_dev(off):
        return (silo, lax.rem(f + off, NF))

    def silo_dev(dy, dx):
        return (lax.rem(y + dy, SIDE) * SIDE + lax.rem(x + dx, SIDE), f)

    barrier = pltpu.get_barrier_semaphore()
    for off in FAR_FIRST:
        pl.semaphore_signal(barrier, inc=1, device_id=feat_dev(off), device_id_type=MESH)
    for k in range(1, SIDE):
        pl.semaphore_signal(barrier, inc=1, device_id=silo_dev(0, k), device_id_type=MESH)
        pl.semaphore_signal(barrier, inc=1, device_id=silo_dev(k, 0), device_id_type=MESH)

    small = [
        pltpu.make_async_copy(observed_in, observed, in_sem.at[0]),
        pltpu.make_async_copy(owner_in, owner, in_sem.at[1]),
    ]
    for cp in small:
        cp.start()

    def loads(b):
        cols = pl.ds(pl.multiple_of(b * W, W), W)
        return (
            pltpu.make_async_copy(components.at[:, cols], xv.at[b, pl.ds(ROWS, K)], ld_sem.at[b, 0]),
            pltpu.make_async_copy(samples.at[:, cols], xv.at[b, pl.ds(0, ROWS)], ld_sem.at[b, 1]),
        )

    def start_load(b, c):
        for cp in loads(b):
            cp.start()
        return c

    lax.fori_loop(0, NB, start_load, 0)
    acc[...] = jnp.zeros_like(acc)
    cnt[0] = jnp.full((8, 128), counts[0].astype(F32), F32)
    for cp in small:
        cp.wait()

    def project(g, c):
        for j in range(GROUP):
            for cp in loads(g * GROUP + j):
                cp.wait()
        proj, gram = acc[:, 0:ROWS], acc[:, ROWS:RK]
        for j in range(GROUP):
            b = g * GROUP + j
            r = dot_nt(xv[b, ROWS:RK, :], xv[b])
            proj = proj + observed[0, b].astype(F32) * r[:, 0:ROWS]
            gram = gram + r[:, ROWS:RK]
        acc[:, 0:ROWS] = proj
        acc[:, ROWS:RK] = gram
        return c

    lax.fori_loop(0, NB // GROUP, project, 0)

    for j in range(NF):
        sbuf[j] = acc[KC * j : KC * (j + 1), :]

    pl.semaphore_wait(barrier, NF - 1 + 2 * (SIDE - 1))

    def rs_copy(off):
        peer = lax.rem(f + off, NF)
        return pltpu.make_async_remote_copy(
            src_ref=sbuf.at[peer], dst_ref=r1.at[off], send_sem=s1_s.at[off],
            recv_sem=s1_r.at[off], device_id=(silo, peer), device_id_type=MESH,
        )

    for off in FAR_FIRST:
        rs_copy(off).start()

    def cnt_copy(k, stage):
        dev = silo_dev(0, k) if stage == 0 else silo_dev(k, 0)
        return pltpu.make_async_remote_copy(
            src_ref=cnt.at[stage], dst_ref=cnt_r.at[stage, k], send_sem=c_s.at[stage, k],
            recv_sem=c_r.at[stage, k], device_id=dev, device_id_type=MESH,
        )

    for k in range(1, SIDE):
        cnt_copy(k, 0).start()

    def invert(d, c):
        block = jnp.int32(0)
        for b in range(NB):
            block = jnp.where(owner[b] == d, jnp.int32(b), block)
        inv[d] = block
        return c

    lax.fori_loop(0, NB, invert, 0)

    total = sbuf[f]
    for off in reversed(FAR_FIRST):
        rs_copy(off).wait_recv()
        total = total + r1[off]
    g2[f] = total

    def ag_copy(off):
        return pltpu.make_async_remote_copy(
            src_ref=g2.at[f], dst_ref=g2.at[f], send_sem=s2_s.at[off],
            recv_sem=s2_r.at[off], device_id=feat_dev(off), device_id_type=MESH,
        )

    for off in FAR_FIRST:
        ag_copy(off).start()

    for k in range(1, SIDE):
        cnt_copy(k, 0).wait_recv()
    cnt[1] = cnt[0] + cnt_r[0, 1] + cnt_r[0, 2] + cnt_r[0, 3]
    for k in range(1, SIDE):
        cnt_copy(k, 1).start()

    for off in reversed(FAR_FIRST):
        ag_copy(off).wait_recv()

    for j in range(NF):
        acc[KC * j : KC * (j + 1), :] = g2[j]
    row = lax.broadcasted_iota(jnp.int32, (K, ROWS), 1)
    proj = jnp.where(row < counts[0], acc[:, 0:ROWS], 0.0)
    eye = lax.broadcasted_iota(jnp.int32, (K, K), 0) == lax.broadcasted_iota(
        jnp.int32, (K, K), 1
    )
    factor = jnp.where(eye, 2.0, 0.0) - acc[:, ROWS:RK]
    q = dot_nn(jnp.concatenate(split(factor, 3), axis=0), proj.astype(BF16))
    q = q[0:K] + q[K : 2 * K] + q[2 * K : 3 * K]
    q_hi, q_lo = split(q, 2)
    lhs[0, :, 0:ROWS] = jnp.zeros((2 * K, ROWS), BF16)
    lhs[1, 0:K, 0:ROWS] = q_hi
    lhs[1, K : 2 * K, 0:ROWS] = q_lo
    both = jnp.concatenate(split(proj, 2), axis=0)
    cross = dot_nt(both, both)
    cross = (
        cross[0:K, 0:K] + (cross[0:K, K : 2 * K] + cross[K : 2 * K, 0:K])
        + cross[K : 2 * K, K : 2 * K]
    )
    c_hi, c_lo = split(-cross, 2)
    for s in range(2):
        lhs[s, 0:K, ROWS:RK] = c_hi
        lhs[s, K : 2 * K, ROWS:RK] = c_lo

    def a_copy(kind, i):
        way = WAY[i]
        k = (2, SIDE - way, way)[kind]
        to = (way, SIDE - way, way)[kind]
        return pltpu.make_async_remote_copy(
            src_ref=ta.at[k, i], dst_ref=ra.at[kind, i], send_sem=a_s.at[kind, i],
            recv_sem=a_r.at[kind, i], device_id=silo_dev(0, to), device_id_type=MESH,
        )

    def b_copy(kind, i):
        way = WAY[i]
        k = (2, SIDE - way, way)[kind]
        to = (way, SIDE - way, way)[kind]
        return pltpu.make_async_remote_copy(
            src_ref=tb.at[k, i], dst_ref=rb.at[kind, i], send_sem=b_s.at[kind, i],
            recv_sem=b_r.at[kind, i], device_id=silo_dev(to, 0), device_id_type=MESH,
        )

    def kind_of(k, i):
        if k == 2:
            return 0
        return 1 if k == SIDE - WAY[i] else None

    for dy, dx in BLOCKS:
        d = lax.rem(y + dy, SIDE) * SIDE + lax.rem(x + dx, SIDE)
        b = inv[d]
        p = dot_nn(lhs[observed[0, b]], xv[b])
        p = p[0:K] + p[K : 2 * K]
        ta[dx, dy] = p[:, 0:HALF]
        if kind_of(dx, dy) is not None:
            a_copy(kind_of(dx, dy), dy).start()
        tb[dy, dx] = p[:, HALF:W]
        if kind_of(dy, dx) is not None:
            b_copy(kind_of(dy, dx), dx).start()

    for i in (2, 3, 1, 0):
        k = WAY[i]
        a_copy(0, i).wait_recv()
        ta[k, i] += ra[0, i]
        a_copy(2, i).start()
        b_copy(0, i).wait_recv()
        tb[k, i] += rb[0, i]
        b_copy(2, i).start()

    def a2_copy(k):
        return pltpu.make_async_remote_copy(
            src_ref=sa.at[k], dst_ref=r2a.at[k], send_sem=a2_s.at[k],
            recv_sem=a2_r.at[k], device_id=silo_dev(k, 0), device_id_type=MESH,
        )

    def b2_copy(k):
        return pltpu.make_async_remote_copy(
            src_ref=sb.at[k], dst_ref=r2b.at[k], send_sem=b2_s.at[k],
            recv_sem=b2_r.at[k], device_id=silo_dev(0, k), device_id_type=MESH,
        )

    for i in (2, 3, 1, 0):
        a_copy(1, i).wait_recv()
        a_copy(2, i).wait_recv()
        sa[i] = ta[0, i] + ra[1, i] + ra[2, i]
        if i:
            a2_copy(i).start()
        b_copy(1, i).wait_recv()
        b_copy(2, i).wait_recv()
        sb[i] = tb[0, i] + rb[1, i] + rb[2, i]
        if i:
            b2_copy(i).start()

    for k in range(1, SIDE):
        cnt_copy(k, 1).wait_recv()
    rows = cnt[1] + cnt_r[1, 1] + cnt_r[1, 2] + cnt_r[1, 3]
    scale = -2.0 / rows[0:1, 0:1]
    for k in range(1, SIDE):
        a2_copy(k).wait_recv()
        b2_copy(k).wait_recv()
    out[:, 0:HALF] = scale * (sa[0] + r2a[1] + r2a[2] + r2a[3])
    out[:, HALF:W] = scale * (sb[0] + r2b[1] + r2b[2] + r2b[3])

    for off in range(1, NF):
        rs_copy(off).wait_send()
        ag_copy(off).wait_send()
    for k in range(1, SIDE):
        cnt_copy(k, 0).wait_send()
        cnt_copy(k, 1).wait_send()
        a2_copy(k).wait_send()
        b2_copy(k).wait_send()
    for i in range(SIDE):
        for kind in range(3):
            a_copy(kind, i).wait_send()
            b_copy(kind, i).wait_send()


def local(samples, components, row_counts, observed, block_owner):
    dma = pltpu.SemaphoreType.DMA
    samples, components, observed, block_owner = (
        pltpu.with_memory_space_constraint(a, pltpu.HBM)
        for a in (samples, components, observed, block_owner)
    )
    return pl.pallas_call(
        kernel,
        name="pca_grad",
        out_shape=jax.ShapeDtypeStruct((K, W), F32),
        in_specs=[
            pl.BlockSpec(memory_space=pl.ANY),
            pl.BlockSpec(memory_space=pl.ANY),
            pl.BlockSpec(memory_space=pltpu.SMEM),
            pl.BlockSpec(memory_space=pl.ANY),
            pl.BlockSpec(memory_space=pl.ANY),
        ],
        out_specs=pl.BlockSpec(memory_space=pltpu.VMEM),
        scratch_shapes=[
            pltpu.SMEM((1, NB), jnp.int32),
            pltpu.SMEM((NB,), jnp.int32),
            pltpu.VMEM((NB, RK, W), BF16),
            pltpu.VMEM((K, CW), F32),
            pltpu.VMEM((NF, KC, CW), F32),
            pltpu.VMEM((NF, KC, CW), F32),
            pltpu.VMEM((NF, KC, CW), F32),
            pltpu.SMEM((NB,), jnp.int32),
            pltpu.VMEM((2, 2 * K, RK), BF16),
            pltpu.VMEM((2, 8, 128), F32),
            pltpu.VMEM((2, SIDE, 8, 128), F32),
            pltpu.VMEM((SIDE, SIDE, K, HALF), F32),
            pltpu.VMEM((SIDE, SIDE, K, HALF), F32),
            pltpu.VMEM((3, SIDE, K, HALF), F32),
            pltpu.VMEM((3, SIDE, K, HALF), F32),
            pltpu.VMEM((SIDE, K, HALF), F32),
            pltpu.VMEM((SIDE, K, HALF), F32),
            pltpu.VMEM((SIDE, K, HALF), F32),
            pltpu.VMEM((SIDE, K, HALF), F32),
            dma((2,)), dma((NB, 2)),
            dma((NF,)), dma((NF,)), dma((NF,)), dma((NF,)),
            dma((2, SIDE)), dma((2, SIDE)),
            dma((3, SIDE)), dma((3, SIDE)),
            dma((3, SIDE)), dma((3, SIDE)),
            dma((SIDE,)), dma((SIDE,)), dma((SIDE,)), dma((SIDE,)),
        ],
        compiler_params=pltpu.CompilerParams(
            collective_id=0, has_side_effects=True, vmem_limit_bytes=40 * 2**20
        ),
        cost_estimate=pl.CostEstimate(
            flops=4 * ROWS * K * NB * W, bytes_accessed=10 * 2**20, transcendentals=0
        ),
    )(samples, components, row_counts, observed, block_owner)


def solution(mesh):
    in_specs = (P("silo", "feat"), P(None, "feat"), P("silo"), P("silo", "feat"), P("feat"))
    out_specs = P(None, ("silo", "feat"))
    return jax.shard_map(local, mesh=mesh, in_specs=in_specs, out_specs=out_specs, check_vma=False)
```

```python
import jax
import jax.numpy as jnp
from jax import lax
from jax.experimental import pallas as pl
from jax.experimental.pallas import tpu as pltpu
from jax.sharding import PartitionSpec as P

MESH = pl.DeviceIdType.MESH
F32 = jnp.float32
BF16 = jnp.bfloat16
SIDE = 4
NF = 16
NB = 16
W = 512
HALF = 256
ROWS = 512
K = 64
RK = ROWS + K
KC = K // NF
LANES = (384, 256)
GROUP = 4

FAR_FIRST = [8, 9, 7, 6, 10, 11, 5, 4, 12, 13, 3, 2, 14, 15, 1]
BLOCKS = [
    (2, 2), (3, 2), (2, 3), (1, 2), (2, 1), (0, 2), (2, 0), (3, 1),
    (1, 3), (0, 1), (1, 0), (3, 3), (1, 1), (0, 3), (3, 0), (0, 0),
]
WAY = {2: 1, 1: 1, 3: SIDE - 1, 0: SIDE - 1}


def dot_nt(a, b):
    return lax.dot_general(a, b, (((1,), (1,)), ((), ())), preferred_element_type=F32)


def dot_nn(a, b):
    return jnp.dot(a, b, preferred_element_type=F32)


def split(v, terms):
    out = []
    for _ in range(terms):
        t = v.astype(BF16)
        out.append(t)
        v = v - t.astype(F32)
    return out


def kernel(
    samples, components, counts, observed_in, owner_in, out,
    observed, owner, xs, seen, acc_0, acc_1, sbuf_0, sbuf_1, r1_0, r1_1, g2_0, g2_1, inv, lhs, cnt, cnt_r,
    ta, tb, ra, rb, sa, sb, r2a, r2b,
    in_sem, comp_sem, ld_sem, s1_s, s1_r, s2_s, s2_r, c_s, c_r,
    a_s, a_r, b_s, b_r, a2_s, a2_r, b2_s, b2_r,
):
    acc, sbuf, r1, g2 = (acc_0, acc_1), (sbuf_0, sbuf_1), (r1_0, r1_1), (g2_0, g2_1)
    silo = lax.axis_index("silo")
    f = lax.axis_index("feat")
    y, x = silo // SIDE, silo % SIDE

    def feat_dev(off):
        return (silo, lax.rem(f + off, NF))

    def silo_dev(dy, dx):
        return (lax.rem(y + dy, SIDE) * SIDE + lax.rem(x + dx, SIDE), f)

    small = [
        pltpu.make_async_copy(observed_in, observed, in_sem.at[0]),
        pltpu.make_async_copy(owner_in, owner, in_sem.at[1]),
    ]
    load_comp = pltpu.make_async_copy(components, xs.at[pl.ds(ROWS, K)], comp_sem.at[0])

    def columns(g):
        return pl.ds(pl.multiple_of(g * GROUP * W, GROUP * W), GROUP * W)

    def load(h, g):
        part = (pl.ds(h * HALF, HALF), columns(g))
        return pltpu.make_async_copy(samples.at[part], xs.at[part], ld_sem.at[h, g])

    for cp in small:
        cp.start()
    load_comp.start()
    for g in range(NB // GROUP):
        load(0, g).start()

    barrier = pltpu.get_barrier_semaphore()
    for off in FAR_FIRST:
        pl.semaphore_signal(barrier, inc=1, device_id=feat_dev(off), device_id_type=MESH)
    for k in range(1, SIDE):
        pl.semaphore_signal(barrier, inc=1, device_id=silo_dev(0, k), device_id_type=MESH)
        pl.semaphore_signal(barrier, inc=1, device_id=silo_dev(k, 0), device_id_type=MESH)

    cnt[0] = jnp.full((8, 128), counts[0].astype(F32), F32)
    for cp in small:
        cp.wait()
    load_comp.wait()

    for b in range(NB):
        cols = slice(b * W, (b + 1) * W)
        seen[:, cols] = xs[ROWS:RK, cols] * observed[0, b].astype(F32).astype(BF16)

    def rs_copy(h, off):
        peer = lax.rem(f + off, NF)
        return pltpu.make_async_remote_copy(
            src_ref=sbuf[h].at[peer], dst_ref=r1[h].at[off], send_sem=s1_s.at[h, off],
            recv_sem=s1_r.at[h, off], device_id=(silo, peer), device_id_type=MESH,
        )

    def ag_copy(h, off):
        return pltpu.make_async_remote_copy(
            src_ref=g2[h].at[f], dst_ref=g2[h].at[f], send_sem=s2_s.at[h, off],
            recv_sem=s2_r.at[h, off], device_id=feat_dev(off), device_id_type=MESH,
        )

    acc[0][:, 0:HALF] = jnp.zeros((K, HALF), F32)
    acc[0][:, HALF : HALF + K] = dot_nt(xs[ROWS:RK, :], xs[ROWS:RK, :])
    acc[1][...] = jnp.zeros((K, HALF), F32)
    for h in range(2):

        def project(g, c):
            load(h, g).wait()
            if h == 0:
                load(1, g).start()
            acc[h][:, 0:HALF] += dot_nt(
                seen[:, columns(g)], xs[h * HALF : (h + 1) * HALF, columns(g)]
            )
            return c

        lax.fori_loop(0, NB // GROUP, project, 0)
        for j in range(NF):
            sbuf[h][j] = acc[h][KC * j : KC * (j + 1), :]
        if h == 0:
            pl.semaphore_wait(barrier, NF - 1 + 2 * (SIDE - 1))
        for off in FAR_FIRST:
            rs_copy(h, off).start()

    def cnt_copy(k, stage):
        dev = silo_dev(0, k) if stage == 0 else silo_dev(k, 0)
        return pltpu.make_async_remote_copy(
            src_ref=cnt.at[stage], dst_ref=cnt_r.at[stage, k], send_sem=c_s.at[stage, k],
            recv_sem=c_r.at[stage, k], device_id=dev, device_id_type=MESH,
        )

    for k in range(1, SIDE):
        cnt_copy(k, 0).start()

    def invert(d, c):
        block = jnp.int32(0)
        for b in range(NB):
            block = jnp.where(owner[b] == d, jnp.int32(b), block)
        inv[d] = block
        return c

    lax.fori_loop(0, NB, invert, 0)

    for h in range(2):
        total = sbuf[h][f]
        for off in reversed(FAR_FIRST):
            rs_copy(h, off).wait_recv()
            total = total + r1[h][off]
        g2[h][f] = total
        for off in FAR_FIRST:
            ag_copy(h, off).start()

    for k in range(1, SIDE):
        cnt_copy(k, 0).wait_recv()
    cnt[1] = cnt[0] + cnt_r[0, 1] + cnt_r[0, 2] + cnt_r[0, 3]
    for k in range(1, SIDE):
        cnt_copy(k, 1).start()

    lhs[0, :, 0:ROWS] = jnp.zeros((2 * K, ROWS), BF16)
    cross = jnp.zeros((2 * K, 2 * K), F32)
    for h in range(2):
        for off in reversed(FAR_FIRST):
            ag_copy(h, off).wait_recv()
        for j in range(NF):
            acc[h][KC * j : KC * (j + 1), :] = g2[h][j]
        if h == 0:
            eye = lax.broadcasted_iota(jnp.int32, (K, K), 0) == lax.broadcasted_iota(
                jnp.int32, (K, K), 1
            )
            factor = jnp.where(eye, 2.0, 0.0) - acc[0][:, HALF : HALF + K]
            factor = jnp.concatenate(split(factor, 3), axis=0)
        row = lax.broadcasted_iota(jnp.int32, (K, HALF), 1) + h * HALF
        proj = jnp.where(row < counts[0], acc[h][:, 0:HALF], 0.0)
        both = split(proj, 2)
        q = dot_nn(factor, both[0])
        q_hi, q_lo = split(q[0:K] + q[K : 2 * K] + q[2 * K : 3 * K], 2)
        lhs[1, 0:K, h * HALF : (h + 1) * HALF] = q_hi
        lhs[1, K : 2 * K, h * HALF : (h + 1) * HALF] = q_lo
        both = jnp.concatenate(both, axis=0)
        cross = cross + dot_nt(both, both)
    cross = (
        cross[0:K, 0:K] + (cross[0:K, K : 2 * K] + cross[K : 2 * K, 0:K])
        + cross[K : 2 * K, K : 2 * K]
    )
    c_hi, c_lo = split(-cross, 2)
    for s in range(2):
        lhs[s, 0:K, ROWS:RK] = c_hi
        lhs[s, K : 2 * K, ROWS:RK] = c_lo

    def a_copy(kind, i):
        way = WAY[i]
        k = (2, SIDE - way, way)[kind]
        to = (way, SIDE - way, way)[kind]
        return pltpu.make_async_remote_copy(
            src_ref=ta.at[k, i], dst_ref=ra.at[kind, i], send_sem=a_s.at[kind, i],
            recv_sem=a_r.at[kind, i], device_id=silo_dev(0, to), device_id_type=MESH,
        )

    def b_copy(kind, i):
        way = WAY[i]
        k = (2, SIDE - way, way)[kind]
        to = (way, SIDE - way, way)[kind]
        return pltpu.make_async_remote_copy(
            src_ref=tb.at[k, i], dst_ref=rb.at[kind, i], send_sem=b_s.at[kind, i],
            recv_sem=b_r.at[kind, i], device_id=silo_dev(to, 0), device_id_type=MESH,
        )

    def kind_of(k, i):
        if k == 2:
            return 0
        return None

    for dy, dx in BLOCKS:
        d = lax.rem(y + dy, SIDE) * SIDE + lax.rem(x + dx, SIDE)
        b = inv[d]
        cols = pl.ds(b * W, W)
        p = dot_nn(lhs[observed[0, b]], xs[:, cols])
        p = p[0:K] + p[K : 2 * K]
        ta[dx, dy] = p[:, 0:HALF]
        if kind_of(dx, dy) is not None:
            a_copy(kind_of(dx, dy), dy).start()
        tb[dy, dx] = p[:, HALF:W]
        if kind_of(dy, dx) is not None:
            b_copy(kind_of(dy, dx), dx).start()

    for i in (2, 3):
        a_copy(0, i).wait_send()
        b_copy(0, i).wait_send()
        a_copy(1, 5 - i).start()
        b_copy(1, 5 - i).start()
    for i in (0, 1):
        a_copy(0, i).wait_send()
        b_copy(0, i).wait_send()
    a_copy(1, 1).start()
    b_copy(1, 1).start()
    for i in (2, 3, 1, 0):
        k = WAY[i]
        a_copy(0, i).wait_recv()
        ta[k, i] += ra[0, i]
        a_copy(2, i).start()
        b_copy(0, i).wait_recv()
        tb[k, i] += rb[0, i]
        b_copy(2, i).start()
    a_copy(1, 0).start()
    b_copy(1, 0).start()

    for h in range(2):
        for off in range(1, NF):
            rs_copy(h, off).wait_send()
            ag_copy(h, off).wait_send()
    for k in range(1, SIDE):
        cnt_copy(k, 0).wait_send()
        cnt_copy(k, 1).wait_send()
        cnt_copy(k, 1).wait_recv()
    rows = cnt[1] + cnt_r[1, 1] + cnt_r[1, 2] + cnt_r[1, 3]
    scale = -2.0 / rows[0:1, 0:1]

    def a2_copy(k):
        return pltpu.make_async_remote_copy(
            src_ref=sa.at[k], dst_ref=r2a.at[k], send_sem=a2_s.at[k],
            recv_sem=a2_r.at[k], device_id=silo_dev(k, 0), device_id_type=MESH,
        )

    def b2_copy(k):
        return pltpu.make_async_remote_copy(
            src_ref=sb.at[k], dst_ref=r2b.at[k], send_sem=b2_s.at[k],
            recv_sem=b2_r.at[k], device_id=silo_dev(0, k), device_id_type=MESH,
        )

    for i in (2, 1, 3, 0):
        a_copy(1, i).wait_recv()
        a_copy(2, i).wait_recv()
        sa[i] = ta[0, i] + ra[1, i] + ra[2, i]
        if i:
            a2_copy(i).start()
        b_copy(1, i).wait_recv()
        b_copy(2, i).wait_recv()
        sb[i] = tb[0, i] + rb[1, i] + rb[2, i]
        if i:
            b2_copy(i).start()

    for i in range(SIDE):
        for kind in range(1, 3):
            a_copy(kind, i).wait_send()
            b_copy(kind, i).wait_send()
    for k in (1, 3, 2):
        a2_copy(k).wait_recv()
        b2_copy(k).wait_recv()
    out[:, 0:HALF] = scale * (sa[0] + r2a[1] + r2a[2] + r2a[3])
    out[:, HALF:W] = scale * (sb[0] + r2b[1] + r2b[2] + r2b[3])

    for k in range(1, SIDE):
        a2_copy(k).wait_send()
        b2_copy(k).wait_send()


def local(samples, components, row_counts, observed, block_owner):
    dma = pltpu.SemaphoreType.DMA
    samples, components, observed, block_owner = (
        pltpu.with_memory_space_constraint(a, pltpu.HBM)
        for a in (samples, components, observed, block_owner)
    )
    return pl.pallas_call(
        kernel,
        name="pca_grad",
        out_shape=jax.ShapeDtypeStruct((K, W), F32),
        in_specs=[
            pl.BlockSpec(memory_space=pl.ANY),
            pl.BlockSpec(memory_space=pl.ANY),
            pl.BlockSpec(memory_space=pltpu.SMEM),
            pl.BlockSpec(memory_space=pl.ANY),
            pl.BlockSpec(memory_space=pl.ANY),
        ],
        out_specs=pl.BlockSpec(memory_space=pltpu.VMEM),
        scratch_shapes=[
            pltpu.SMEM((1, NB), jnp.int32),
            pltpu.SMEM((NB,), jnp.int32),
            pltpu.VMEM((RK, NB * W), BF16),
            pltpu.VMEM((K, NB * W), BF16),
            pltpu.VMEM((K, LANES[0]), F32),
            pltpu.VMEM((K, LANES[1]), F32),
            pltpu.VMEM((NF, KC, LANES[0]), F32),
            pltpu.VMEM((NF, KC, LANES[1]), F32),
            pltpu.VMEM((NF, KC, LANES[0]), F32),
            pltpu.VMEM((NF, KC, LANES[1]), F32),
            pltpu.VMEM((NF, KC, LANES[0]), F32),
            pltpu.VMEM((NF, KC, LANES[1]), F32),
            pltpu.SMEM((NB,), jnp.int32),
            pltpu.VMEM((2, 2 * K, RK), BF16),
            pltpu.VMEM((2, 8, 128), F32),
            pltpu.VMEM((2, SIDE, 8, 128), F32),
            pltpu.VMEM((SIDE, SIDE, K, HALF), F32),
            pltpu.VMEM((SIDE, SIDE, K, HALF), F32),
            pltpu.VMEM((3, SIDE, K, HALF), F32),
            pltpu.VMEM((3, SIDE, K, HALF), F32),
            pltpu.VMEM((SIDE, K, HALF), F32),
            pltpu.VMEM((SIDE, K, HALF), F32),
            pltpu.VMEM((SIDE, K, HALF), F32),
            pltpu.VMEM((SIDE, K, HALF), F32),
            dma((2,)), dma((1,)), dma((2, NB // GROUP)),
            dma((2, NF)), dma((2, NF)), dma((2, NF)), dma((2, NF)),
            dma((2, SIDE)), dma((2, SIDE)),
            dma((3, SIDE)), dma((3, SIDE)),
            dma((3, SIDE)), dma((3, SIDE)),
            dma((SIDE,)), dma((SIDE,)), dma((SIDE,)), dma((SIDE,)),
        ],
        compiler_params=pltpu.CompilerParams(
            collective_id=0, has_side_effects=True, vmem_limit_bytes=40 * 2**20
        ),
        cost_estimate=pl.CostEstimate(
            flops=4 * ROWS * K * NB * W, bytes_accessed=10 * 2**20, transcendentals=0
        ),
    )(samples, components, row_counts, observed, block_owner)


def solution(mesh):
    in_specs = (P("silo", "feat"), P(None, "feat"), P("silo"), P("silo", "feat"), P("feat"))
    out_specs = P(None, ("silo", "feat"))
    return jax.shard_map(local, mesh=mesh, in_specs=in_specs, out_specs=out_specs, check_vma=False)
```

```python
import jax
import jax.numpy as jnp
from jax import lax
from jax.experimental import pallas as pl
from jax.experimental.pallas import tpu as pltpu
from jax.sharding import PartitionSpec as P

MESH = pl.DeviceIdType.MESH
F32 = jnp.float32
BF16 = jnp.bfloat16
SIDE = 4
NF = 16
NB = 16
W = 512
HALF = 256
ROWS = 512
K = 64
RK = ROWS + K
KC = K // NF
LANES = (384, 256)
GROUP = 8

FAR_FIRST = [8, 9, 7, 6, 10, 11, 5, 4, 12, 13, 3, 2, 14, 15, 1]
BLOCKS = [
    (2, 2), (3, 2), (2, 3), (1, 2), (2, 1), (0, 2), (2, 0), (3, 1),
    (1, 3), (0, 1), (1, 0), (3, 3), (1, 1), (0, 3), (3, 0), (0, 0),
]
WAY = {2: 1, 1: 1, 3: SIDE - 1, 0: SIDE - 1}


def dot_nt(a, b):
    return lax.dot_general(a, b, (((1,), (1,)), ((), ())), preferred_element_type=F32)


def dot_nn(a, b):
    return jnp.dot(a, b, preferred_element_type=F32)


def split(v, terms):
    out = []
    for _ in range(terms):
        t = v.astype(BF16)
        out.append(t)
        v = v - t.astype(F32)
    return out


def kernel(
    samples, components, counts, observed_in, owner_in, out,
    observed, owner, xs, seen, acc_0, acc_1, sbuf_0, sbuf_1, r1_0, r1_1, g2_0, g2_1, inv, lhs, cnt, cnt_r,
    ta, tb, ra, rb, sa, sb, r2a, r2b,
    in_sem, comp_sem, ld_sem, s1_s, s1_r, s2_s, s2_r, c_s, c_r,
    a_s, a_r, b_s, b_r, a2_s, a2_r, b2_s, b2_r,
):
    acc, sbuf, r1, g2 = (acc_0, acc_1), (sbuf_0, sbuf_1), (r1_0, r1_1), (g2_0, g2_1)
    silo = lax.axis_index("silo")
    f = lax.axis_index("feat")
    y, x = silo // SIDE, silo % SIDE

    def feat_dev(off):
        return (silo, lax.rem(f + off, NF))

    def silo_dev(dy, dx):
        return (lax.rem(y + dy, SIDE) * SIDE + lax.rem(x + dx, SIDE), f)

    small = [
        pltpu.make_async_copy(observed_in, observed, in_sem.at[0]),
        pltpu.make_async_copy(owner_in, owner, in_sem.at[1]),
    ]
    load_comp = pltpu.make_async_copy(components, xs.at[pl.ds(ROWS, K)], comp_sem.at[0])

    def columns(g):
        return pl.ds(pl.multiple_of(g * GROUP * W, GROUP * W), GROUP * W)

    def load(h, g):
        part = (pl.ds(h * HALF, HALF), columns(g))
        return pltpu.make_async_copy(samples.at[part], xs.at[part], ld_sem.at[h, g])

    for cp in small:
        cp.start()
    load_comp.start()
    for g in range(NB // GROUP):
        load(0, g).start()
    for g in range(NB // GROUP):
        load(1, g).start()

    barrier = pltpu.get_barrier_semaphore()
    for off in FAR_FIRST:
        pl.semaphore_signal(barrier, inc=1, device_id=feat_dev(off), device_id_type=MESH)
    for k in range(1, SIDE):
        pl.semaphore_signal(barrier, inc=1, device_id=silo_dev(0, k), device_id_type=MESH)
        pl.semaphore_signal(barrier, inc=1, device_id=silo_dev(k, 0), device_id_type=MESH)

    cnt[0] = jnp.full((8, 128), counts[0].astype(F32), F32)
    for cp in small:
        cp.wait()
    load_comp.wait()

    for b in range(NB):
        cols = slice(b * W, (b + 1) * W)
        seen[:, cols] = xs[ROWS:RK, cols] * observed[0, b].astype(F32).astype(BF16)

    def rs_copy(h, off):
        peer = lax.rem(f + off, NF)
        return pltpu.make_async_remote_copy(
            src_ref=sbuf[h].at[peer], dst_ref=r1[h].at[off], send_sem=s1_s.at[h, off],
            recv_sem=s1_r.at[h, off], device_id=(silo, peer), device_id_type=MESH,
        )

    def ag_copy(h, off):
        return pltpu.make_async_remote_copy(
            src_ref=g2[h].at[f], dst_ref=g2[h].at[f], send_sem=s2_s.at[h, off],
            recv_sem=s2_r.at[h, off], device_id=feat_dev(off), device_id_type=MESH,
        )

    acc[0][:, 0:HALF] = jnp.zeros((K, HALF), F32)
    acc[0][:, HALF : HALF + K] = dot_nt(xs[ROWS:RK, :], xs[ROWS:RK, :])
    acc[1][...] = jnp.zeros((K, HALF), F32)
    for h in range(2):

        def project(g, c):
            load(h, g).wait()
            acc[h][:, 0:HALF] += dot_nt(
                seen[:, columns(g)], xs[h * HALF : (h + 1) * HALF, columns(g)]
            )
            return c

        lax.fori_loop(0, NB // GROUP, project, 0)
        for j in range(NF):
            sbuf[h][j] = acc[h][KC * j : KC * (j + 1), :]
        if h == 0:
            pl.semaphore_wait(barrier, NF - 1 + 2 * (SIDE - 1))
        for off in FAR_FIRST:
            rs_copy(h, off).start()

    def cnt_copy(k, stage):
        dev = silo_dev(0, k) if stage == 0 else silo_dev(k, 0)
        return pltpu.make_async_remote_copy(
            src_ref=cnt.at[stage], dst_ref=cnt_r.at[stage, k], send_sem=c_s.at[stage, k],
            recv_sem=c_r.at[stage, k], device_id=dev, device_id_type=MESH,
        )

    for k in range(1, SIDE):
        cnt_copy(k, 0).start()

    def invert(d, c):
        block = jnp.int32(0)
        for b in range(NB):
            block = jnp.where(owner[b] == d, jnp.int32(b), block)
        inv[d] = block
        return c

    lax.fori_loop(0, NB, invert, 0)

    for h in range(2):
        total = sbuf[h][f]
        for off in reversed(FAR_FIRST):
            rs_copy(h, off).wait_recv()
            total = total + r1[h][off]
        g2[h][f] = total
        for off in FAR_FIRST:
            ag_copy(h, off).start()

    for k in range(1, SIDE):
        cnt_copy(k, 0).wait_recv()
    cnt[1] = cnt[0] + cnt_r[0, 1] + cnt_r[0, 2] + cnt_r[0, 3]
    for k in range(1, SIDE):
        cnt_copy(k, 1).start()

    lhs[0, :, 0:ROWS] = jnp.zeros((2 * K, ROWS), BF16)
    cross = jnp.zeros((K, K), F32)
    for h in range(2):
        for off in reversed(FAR_FIRST):
            ag_copy(h, off).wait_recv()
        for j in range(NF):
            acc[h][KC * j : KC * (j + 1), :] = g2[h][j]
        if h == 0:
            eye = lax.broadcasted_iota(jnp.int32, (K, K), 0) == lax.broadcasted_iota(
                jnp.int32, (K, K), 1
            )
            factor = jnp.where(eye, 2.0, 0.0) - acc[0][:, HALF : HALF + K]
            factor = jnp.concatenate(split(factor, 3), axis=1)
        row = lax.broadcasted_iota(jnp.int32, (K, HALF), 1) + h * HALF
        proj = jnp.where(row < counts[0], acc[h][:, 0:HALF], 0.0)
        hi, lo = split(proj, 2)
        q = dot_nn(factor, jnp.concatenate([hi, hi, hi], axis=0))
        q_hi, q_lo = split(q, 2)
        lhs[1, 0:K, h * HALF : (h + 1) * HALF] = q_hi
        lhs[1, K : 2 * K, h * HALF : (h + 1) * HALF] = q_lo
        cross = cross + dot_nt(
            jnp.concatenate([hi, hi, lo, lo], axis=1), jnp.concatenate([hi, lo, hi, lo], axis=1)
        )
    c_hi, c_lo = split(-cross, 2)
    for s in range(2):
        lhs[s, 0:K, ROWS:RK] = c_hi
        lhs[s, K : 2 * K, ROWS:RK] = c_lo

    def a_copy(kind, i):
        way = WAY[i]
        k = (2, SIDE - way, way)[kind]
        to = (way, SIDE - way, way)[kind]
        return pltpu.make_async_remote_copy(
            src_ref=ta.at[k, i], dst_ref=ra.at[kind, i], send_sem=a_s.at[kind, i],
            recv_sem=a_r.at[kind, i], device_id=silo_dev(0, to), device_id_type=MESH,
        )

    def b_copy(kind, i):
        way = WAY[i]
        k = (2, SIDE - way, way)[kind]
        to = (way, SIDE - way, way)[kind]
        return pltpu.make_async_remote_copy(
            src_ref=tb.at[k, i], dst_ref=rb.at[kind, i], send_sem=b_s.at[kind, i],
            recv_sem=b_r.at[kind, i], device_id=silo_dev(to, 0), device_id_type=MESH,
        )

    def send(kind, *rows):
        for i in rows:
            a_copy(kind, i).start()
            b_copy(kind, i).start()

    def sent(kind, *rows):
        for i in rows:
            a_copy(kind, i).wait_send()
            b_copy(kind, i).wait_send()

    def relay(*rows):
        for i in rows:
            k = WAY[i]
            a_copy(0, i).wait_recv()
            ta[k, i] += ra[0, i]
            a_copy(2, i).start()
            b_copy(0, i).wait_recv()
            tb[k, i] += rb[0, i]
            b_copy(2, i).start()

    for dy, dx in BLOCKS:
        d = lax.rem(y + dy, SIDE) * SIDE + lax.rem(x + dx, SIDE)
        b = inv[d]
        p = dot_nn(lhs[observed[0, b]], xs[:, pl.ds(b * W, W)])
        p = p[0:K] + p[K : 2 * K]
        ta[dx, dy] = p[:, 0:HALF]
        tb[dy, dx] = p[:, HALF:W]
        if dx == 2 and dy in (2, 3, 1, 0):
            a_copy(0, dy).start()
        if dy == 2 and dx in (2, 3, 1, 0):
            b_copy(0, dx).start()
    send(1, 3, 2)
    sent(0, 2, 3)
    sent(0, 1, 0)
    send(1, 1)
    relay(2, 3, 1, 0)
    send(1, 0)

    for h in range(2):
        for off in range(1, NF):
            rs_copy(h, off).wait_send()
            ag_copy(h, off).wait_send()
    for k in range(1, SIDE):
        cnt_copy(k, 0).wait_send()
        cnt_copy(k, 1).wait_send()
        cnt_copy(k, 1).wait_recv()
    rows = cnt[1] + cnt_r[1, 1] + cnt_r[1, 2] + cnt_r[1, 3]
    scale = -2.0 / rows[0:1, 0:1]

    def a2_copy(k):
        return pltpu.make_async_remote_copy(
            src_ref=sa.at[k], dst_ref=r2a.at[k], send_sem=a2_s.at[k],
            recv_sem=a2_r.at[k], device_id=silo_dev(k, 0), device_id_type=MESH,
        )

    def b2_copy(k):
        return pltpu.make_async_remote_copy(
            src_ref=sb.at[k], dst_ref=r2b.at[k], send_sem=b2_s.at[k],
            recv_sem=b2_r.at[k], device_id=silo_dev(0, k), device_id_type=MESH,
        )

    def first_sum(i):
        a_copy(1, i).wait_recv()
        a_copy(2, i).wait_recv()
        sa[i] = ta[0, i] + ra[1, i] + ra[2, i]
        if i:
            a2_copy(i).start()
        b_copy(1, i).wait_recv()
        b_copy(2, i).wait_recv()
        sb[i] = tb[0, i] + rb[1, i] + rb[2, i]
        if i:
            b2_copy(i).start()

    first_sum(2)
    first_sum(3)
    first_sum(1)
    first_sum(0)

    sent(1, 0, 1, 2, 3)
    sent(2, 0, 1, 2, 3)
    for k in (1, 3, 2):
        a2_copy(k).wait_recv()
        b2_copy(k).wait_recv()
    out[:, 0:HALF] = scale * (sa[0] + r2a[1] + r2a[2] + r2a[3])
    out[:, HALF:W] = scale * (sb[0] + r2b[1] + r2b[2] + r2b[3])

    for k in range(1, SIDE):
        a2_copy(k).wait_send()
        b2_copy(k).wait_send()


def local(samples, components, row_counts, observed, block_owner):
    dma = pltpu.SemaphoreType.DMA
    samples, components, observed, block_owner = (
        pltpu.with_memory_space_constraint(a, pltpu.HBM)
        for a in (samples, components, observed, block_owner)
    )
    return pl.pallas_call(
        kernel,
        name="pca_grad",
        out_shape=jax.ShapeDtypeStruct((K, W), F32),
        in_specs=[
            pl.BlockSpec(memory_space=pl.ANY),
            pl.BlockSpec(memory_space=pl.ANY),
            pl.BlockSpec(memory_space=pltpu.SMEM),
            pl.BlockSpec(memory_space=pl.ANY),
            pl.BlockSpec(memory_space=pl.ANY),
        ],
        out_specs=pl.BlockSpec(memory_space=pltpu.VMEM),
        scratch_shapes=[
            pltpu.SMEM((1, NB), jnp.int32),
            pltpu.SMEM((NB,), jnp.int32),
            pltpu.VMEM((RK, NB * W), BF16),
            pltpu.VMEM((K, NB * W), BF16),
            pltpu.VMEM((K, LANES[0]), F32),
            pltpu.VMEM((K, LANES[1]), F32),
            pltpu.VMEM((NF, KC, LANES[0]), F32),
            pltpu.VMEM((NF, KC, LANES[1]), F32),
            pltpu.VMEM((NF, KC, LANES[0]), F32),
            pltpu.VMEM((NF, KC, LANES[1]), F32),
            pltpu.VMEM((NF, KC, LANES[0]), F32),
            pltpu.VMEM((NF, KC, LANES[1]), F32),
            pltpu.SMEM((NB,), jnp.int32),
            pltpu.VMEM((2, 2 * K, RK), BF16),
            pltpu.VMEM((2, 8, 128), F32),
            pltpu.VMEM((2, SIDE, 8, 128), F32),
            pltpu.VMEM((SIDE, SIDE, K, HALF), F32),
            pltpu.VMEM((SIDE, SIDE, K, HALF), F32),
            pltpu.VMEM((3, SIDE, K, HALF), F32),
            pltpu.VMEM((3, SIDE, K, HALF), F32),
            pltpu.VMEM((SIDE, K, HALF), F32),
            pltpu.VMEM((SIDE, K, HALF), F32),
            pltpu.VMEM((SIDE, K, HALF), F32),
            pltpu.VMEM((SIDE, K, HALF), F32),
            dma((2,)), dma((1,)), dma((2, NB // GROUP)),
            dma((2, NF)), dma((2, NF)), dma((2, NF)), dma((2, NF)),
            dma((2, SIDE)), dma((2, SIDE)),
            dma((3, SIDE)), dma((3, SIDE)),
            dma((3, SIDE)), dma((3, SIDE)),
            dma((SIDE,)), dma((SIDE,)), dma((SIDE,)), dma((SIDE,)),
        ],
        compiler_params=pltpu.CompilerParams(
            collective_id=0, has_side_effects=True, vmem_limit_bytes=40 * 2**20
        ),
        cost_estimate=pl.CostEstimate(
            flops=4 * ROWS * K * NB * W, bytes_accessed=10 * 2**20, transcendentals=0
        ),
    )(samples, components, row_counts, observed, block_owner)


def solution(mesh):
    in_specs = (P("silo", "feat"), P(None, "feat"), P("silo"), P("silo", "feat"), P("feat"))
    out_specs = P(None, ("silo", "feat"))
    return jax.shard_map(local, mesh=mesh, in_specs=in_specs, out_specs=out_specs, check_vma=False)
```
